32 devices in a mesh: dp: 2 (over x), pipe: 2 (over core), ctx: 8 (over z, y).
Axes of the slice: x: 2, y: 2, z: 4, core: 2. Of those that a mesh axis runs over, the one named last changes fastest.
Arguments:
- section_input: bfloat16 [2, 2, 1024, 2048], P('dp', 'pipe', 'ctx'), may hold values from -6 to 6
- section_positions: int32 [2, 2, 1024], P('dp', 'pipe', 'ctx'), may hold values from 0 to 1023, as said below
- saved_input: bfloat16 [2, 2, 1024, 2048], P('dp', 'pipe', 'ctx'), may hold values from -6 to 6
- saved_positions: int32 [2, 2, 1024], P('dp', 'pipe', 'ctx'), may hold values from 0 to 1023, as said below
- cotangent: bfloat16 [2, 2, 1024, 2048], P('dp', 'pipe', 'ctx'), may hold values from -6 to 6
- norm_gains: float32 [2, 2, 2, 2048], P(None, 'pipe'), may hold values from -2 to 2
- output_gains: float32 [2, 2, 2048], P(None, 'pipe'), may hold values from 0.25 to 2
- plan: int32 [2, 2, 2], P('dp', 'pipe'), may hold values from 0 to 1
Outputs:
- next_input: bfloat16 [2, 2, 1024, 2048], P('dp', 'pipe', 'ctx')
- upstream_grad: bfloat16 [2, 2, 1024, 2048], P('dp', 'pipe', 'ctx')
- gain_grads: float32 [2, 3, 2048], P('pipe')
The draws below stay inside these ranges and needn't reach their ends.
Inputs may be any that keep to these rules, and one draw needn't show every extreme that they name: `section_positions`: in every sequence the first position is 0 and each later one is either one more than the position before it or 0 (a new document). `saved_positions`: in every sequence the first position is 0 and each later one is either one more than the position before it or 0 (a new document).
All inputs are finite; a program needn't handle non-finite values.
Results may differ from the reference program's by a relative error of at most 0.0075.
Values may be sent and summed in bfloat16 or wider, within the bound.
A program may use at most 64 MiB of HBM per device.

```python
import math
import jax
import jax.numpy as jnp
from jax import lax

HEADS = 16
HEAD_DIM = 128
FEATURES = 2048
WINDOW = 512
TOK_DEV = 128
SEQ_LEN = 1024
N_DP = 2
N_PIPE = 2
N_CTX = 8


def document_positions(key, salt):
    period = min(4 * WINDOW, SEQ_LEN)
    random_starts = jax.random.randint(jax.random.fold_in(key, salt), (N_DP, N_PIPE, SEQ_LEN), 0, 2 * WINDOW) == 0
    offsets = lax.broadcasted_iota(jnp.int32, (N_DP, N_PIPE, SEQ_LEN), 2)
    replica_ids = lax.broadcasted_iota(jnp.int32, (N_DP, N_PIPE, SEQ_LEN), 0)
    section_ids = lax.broadcasted_iota(jnp.int32, (N_DP, N_PIPE, SEQ_LEN), 1)
    kept_whole = (replica_ids == 0) & (section_ids == 0) & (offsets < period)
    starts = random_starts & jnp.logical_not(kept_whole) | (offsets % period == 0)
    latest = lax.cummax(jnp.where(starts, offsets, 0), axis=2)
    return (offsets - latest).astype(jnp.int32)


def draw_section_positions(key, part):
    return document_positions(key, 11)


def draw_saved_positions(key, part):
    return document_positions(key, 23)


def with_ends(drawn, rng, low, high):
    longest = drawn.shape.index(max(drawn.shape))
    spots = []
    for shift in (0, 1):
        where = [jax.random.randint(jax.random.fold_in(rng, axis), (), 0, length) for axis, length in enumerate(drawn.shape)]
        where[longest] = (where[longest] + shift) % drawn.shape[longest]
        spots.append(tuple(where))
    return drawn.at[spots[0]].set(low).at[spots[1]].set(high)


def shard_levels(own_key, dims, pieces, smallest, largest):
    factor_of = 1.0
    for dim, shards_of in pieces:
        steps = jax.random.uniform(jax.random.fold_in(jax.random.fold_in(own_key, 6), dim), (shards_of,), jnp.float32, smallest / len(pieces), largest / len(pieces))
        factor_of = factor_of * jnp.repeat(jnp.exp(steps), dims[dim] // shards_of).reshape((-1,) + (1,) * (len(dims) - 1 - dim))
    return factor_of


def noise(own_key, dims, scale, reach, cuts=(), kind=jnp.bfloat16):
    drawn = jax.random.normal(own_key, dims, jnp.float32) * scale
    if len(cuts) > 0:
        drawn = shard_levels(own_key, dims, cuts, -0.22, 0.18) * drawn
    return jnp.clip(drawn, min=-reach, max=reach).astype(kind)


def setup_inputs(seed: int = 0) -> dict:
    keys = jax.random.split(jax.random.key(seed), 9)
    section_input = noise(keys[0], (N_DP, N_PIPE, SEQ_LEN, FEATURES), 1.0, 6.0, ((0, 2), (1, 2), (2, 8)))
    section_positions = draw_section_positions(jax.random.fold_in(keys[8], 71), 0)
    saved_input = noise(keys[2], (N_DP, N_PIPE, SEQ_LEN, FEATURES), 1.0, 6.0, ((0, 2), (1, 2), (2, 8)))
    saved_positions = draw_saved_positions(jax.random.fold_in(keys[8], 71), 0)
    cotangent = noise(keys[4], (N_DP, N_PIPE, SEQ_LEN, FEATURES), 1.0, 6.0, ((0, 2), (1, 2), (2, 8)))
    norm_gains = jnp.clip(jax.random.uniform(keys[5], (2, N_PIPE, 2, FEATURES), jnp.float32, -2.0, 2.0) * shard_levels(keys[5], (2, N_PIPE, 2, FEATURES), ((1, 2),), -0.4, 0.0), -2.0, 2.0)
    output_gains = jnp.clip(jnp.exp(math.log(2.0) - 2.0794415 * jax.random.uniform(keys[6], (2, N_PIPE, FEATURES), jnp.float32) ** shard_levels(keys[6], (2, N_PIPE, FEATURES), ((1, 2),), -0.2, 0.2)), 0.25, 2.0)
    plan = with_ends(jax.random.randint(keys[7], (N_DP, N_PIPE, 2), 0, 2), jax.random.fold_in(keys[7], 1), 0, 1).astype(jnp.int32)
    return dict(section_input=section_input, section_positions=section_positions, saved_input=saved_input, saved_positions=saved_positions, cotangent=cotangent, norm_gains=norm_gains, output_gains=output_gains, plan=plan)


EPSILON = 1e-06

def as_bfloat(values):
    narrow = lax.optimization_barrier(values.astype(jnp.bfloat16)).astype(jnp.float32)
    return values + lax.stop_gradient(narrow - values)

def attend(key_rows, key_pos, key_ok, gains, query_count):
    total_rows = key_rows.shape[0]
    first_row = total_rows - query_count
    shaped = key_rows.reshape(total_rows, HEADS, HEAD_DIM)
    normed = shaped * lax.rsqrt(lax.optimization_barrier(jnp.mean(shaped * shaped, axis=-1, keepdims=True)) + EPSILON)
    query_gain = gains[0].reshape(HEADS, HEAD_DIM)
    key_gain = gains[1].reshape(HEADS, HEAD_DIM)
    queries = as_bfloat(normed[first_row:] * query_gain)
    key_vecs = as_bfloat(normed * key_gain)
    scores = jnp.einsum('qhe,khe->hqk', queries, key_vecs) / jnp.sqrt(jnp.float32(HEAD_DIM))
    query_ids = first_row + jnp.arange(query_count, dtype=jnp.int32)
    key_ids = jnp.arange(total_rows, dtype=jnp.int32)
    distance = query_ids[:, None] - key_ids[None, :]
    query_pos = key_pos[first_row:]
    allowed = (distance >= 0) & (distance < WINDOW) & (query_pos[:, None] - key_pos[None, :] == distance) & key_ok[None, :]
    weights = jnp.where(allowed[None], jnp.exp(scores), jnp.float32(0.0))
    probability = as_bfloat(weights / lax.optimization_barrier(jnp.sum(weights, axis=-1, keepdims=True)))
    mixture = jnp.einsum('hqk,khe->qhe', probability, shaped)
    return key_rows[first_row:] + mixture.reshape(query_count, FEATURES) * gains[2]

def padded_sequence(rows32, positions):
    padded = jnp.concatenate([jnp.zeros((WINDOW, FEATURES), jnp.float32), rows32], axis=0)
    pos_pad = jnp.concatenate([jnp.zeros((WINDOW,), jnp.int32), positions.astype(jnp.int32)], axis=0)
    valid = jnp.concatenate([jnp.zeros((WINDOW,), bool), jnp.ones((SEQ_LEN,), bool)], axis=0)
    return (padded, pos_pad, valid)

def select_gains(norm_gains, output_gains, lap_index, section_index):
    pair_gains = norm_gains[lap_index, section_index]
    return jnp.concatenate([pair_gains, output_gains[lap_index, section_index][None]], axis=0)

def reference(section_input, section_positions, saved_input, saved_positions, cotangent, norm_gains, output_gains, plan):
    pair_count = N_DP * N_PIPE
    span = WINDOW + TOK_DEV
    piece_len = min(WINDOW, TOK_DEV)
    piece_count = WINDOW // piece_len

    def one_pair(operands):
        inputs, positions, saved_rows, saved_pos, cot_rows, pair_index = operands
        section_index = pair_index % N_PIPE
        replica_index = pair_index // N_PIPE
        forward_gains = select_gains(norm_gains, output_gains, plan[replica_index, section_index, 0], section_index)
        backward_gains = select_gains(norm_gains, output_gains, plan[replica_index, section_index, 1], section_index)
        padded, pos_pad, valid = padded_sequence(inputs.astype(jnp.float32), positions)
        outputs = []
        for shard in range(N_CTX):
            start = shard * TOK_DEV
            outputs.append(attend(padded[start:start + span], pos_pad[start:start + span], valid[start:start + span], forward_gains, TOK_DEV))
        produced = jnp.concatenate(outputs, axis=0).astype(jnp.bfloat16)
        s_pad, s_pos, s_valid = padded_sequence(saved_rows.astype(jnp.float32), saved_pos)
        grad_total = jnp.zeros((WINDOW + SEQ_LEN, FEATURES), jnp.float32)
        gain_total = jnp.zeros((3, FEATURES), jnp.float32)
        for shard in range(N_CTX):
            start = shard * TOK_DEV
            these_pos = s_pos[start:start + span]
            these_ok = s_valid[start:start + span]

            def local_layer(rows, gains):
                return attend(rows, these_pos, these_ok, gains, TOK_DEV)
            _, pullback = jax.vjp(local_layer, s_pad[start:start + span], backward_gains)
            key_grads, gain_grad = pullback(cot_rows[start:start + TOK_DEV].astype(jnp.float32))
            rim = lax.optimization_barrier(key_grads[:WINDOW].astype(jnp.bfloat16)).astype(jnp.float32)
            for piece in range(piece_count):
                lo = start + piece * piece_len
                grad_total = grad_total.at[lo:lo + piece_len].add(rim[piece * piece_len:(piece + 1) * piece_len])
            grad_total = grad_total.at[start + WINDOW:start + span].add(key_grads[WINDOW:])
            gain_total = gain_total + gain_grad
        return (produced, grad_total[WINDOW:].astype(jnp.bfloat16), gain_total)
    produced, row_grads, gain_grad = lax.map(one_pair, (section_input.reshape(pair_count, SEQ_LEN, FEATURES), section_positions.reshape(pair_count, SEQ_LEN), saved_input.reshape(pair_count, SEQ_LEN, FEATURES), saved_positions.reshape(pair_count, SEQ_LEN), cotangent.reshape(pair_count, SEQ_LEN, FEATURES), jnp.arange(pair_count, dtype=jnp.int32)))
    produced = produced.reshape(N_DP, N_PIPE, SEQ_LEN, FEATURES)
    row_grads = row_grads.reshape(N_DP, N_PIPE, SEQ_LEN, FEATURES)
    next_input = jnp.roll(produced, 1, axis=1)
    upstream_grad = jnp.roll(row_grads, -1, axis=1)
    gain_grads = lax.optimization_barrier(jnp.sum(gain_grad.reshape(N_DP, N_PIPE, 3, FEATURES), axis=0)) / jnp.float32(TOK_DEV)
    return (next_input, upstream_grad, gain_grads)
```

```python
import functools

import jax
import jax.numpy as jnp
from jax import lax
from jax.experimental import pallas as pl
from jax.experimental.pallas import tpu as pltpu
from jax.sharding import PartitionSpec as P

HEADS = 16
HEAD_DIM = 128
FEATURES = 2048
WINDOW = 512
TOK = 128
REACH = WINDOW // TOK
SPAN = WINDOW + TOK
CHUNKS = 4
WIDTH = FEATURES // CHUNKS
CHUNK_HEADS = HEADS // CHUNKS
EPSILON = 1e-06
SCALE = HEAD_DIM**-0.5
MESH = pl.DeviceIdType.MESH
F32 = jnp.float32
BF16 = jnp.bfloat16
A, B, C, D = range(4)


def sum_stages(sizes):
    stages = []
    for axis in ("dp", "ctx"):
        left, stride = sizes[axis], 1
        while left > 1:
            factor = next(f for f in range(2, left + 1) if left % f == 0)
            stages.append((axis, stride, factor))
            left //= factor
            stride *= factor
    return stages


def slot(reach):
    return (REACH - reach) * TOK


def dot(left, right, left_dim, right_dim):
    return lax.dot_general(
        left, right, (((left_dim,), (right_dim,)), ((), ())), preferred_element_type=F32
    )


def kernel(
    sizes,
    sec_ref,
    sec_pos,
    sav_ref,
    sav_pos,
    cot_ref,
    norm_ref,
    outg_ref,
    plan_ref,
    next_ref,
    up_ref,
    total_ref,
    keys,
    cot,
    gains,
    masks,
    grads,
    own,
    from_partner,
    from_z4,
    from_z2,
    produced,
    dx,
    sums,
    load_sem,
    key_send,
    key_recv,
    grad_send,
    grad_recv,
    out_send,
    out_recv,
    sum_send,
    sum_recv,
):
    n = sizes["ctx"]
    c = lax.axis_index("ctx")
    odd = lax.rem(c, 2)
    even = odd == 0
    partner = c + 1 - 2 * odd
    pipe = lax.axis_index("pipe")
    after = lax.rem(pipe + 1, sizes["pipe"])
    before = lax.rem(pipe + sizes["pipe"] - 1, sizes["pipe"])
    up, down = c + 2 < n, c >= 2
    stages = sum_stages(sizes)

    def rows(first):
        if isinstance(first, int):
            return pl.ds(first, TOK)
        return pl.ds(pl.multiple_of(first, TOK), TOK)

    def columns(j):
        return pl.ds(pl.multiple_of(j * WIDTH, WIDTH), WIDTH)

    def load(which, j):
        source = (sav_ref, sec_ref, cot_ref)[which]
        target = cot.at[j] if which == 2 else keys.at[which, j, rows(WINDOW)]
        return pltpu.make_async_copy(source.at[:, columns(j)], target, load_sem.at[which, j])

    def key_copy(t, kind, j):
        if kind == A:
            source, target, device = slot(0), slot(2), c + 2
        elif kind == B:
            source, target, device = slot(2), slot(4), c + 2
        elif kind == C:
            source, target, device = jnp.where(even, slot(0), slot(2)), slot(1), partner
        else:
            source, target, device = jnp.where(even, slot(2), slot(4)), slot(3), partner
        return pltpu.make_async_remote_copy(
            src_ref=keys.at[t, j, rows(source)],
            dst_ref=keys.at[t, j, rows(target)],
            send_sem=key_send.at[t, kind, j],
            recv_sem=key_recv.at[t, kind, j],
            device_id={"ctx": device},
            device_id_type=MESH,
        )

    sends_key = (up, up & down, even | down, c >= 2 + 2 * odd)
    gets_key = (c >= 2, c >= 4, c >= 1, c >= 3)

    def grad_copy(kind, j):
        if kind < 2:
            source, target, device = slot((1, 3)[kind]), from_partner.at[kind, j], partner
        else:
            source, target, device = slot((4, 2)[kind - 2]), (from_z4, from_z2)[kind - 2].at[j], c - 2
        return pltpu.make_async_remote_copy(
            src_ref=grads.at[j, rows(source)],
            dst_ref=target,
            send_sem=grad_send.at[kind, j],
            recv_sem=grad_recv.at[kind, j],
            device_id={"ctx": device},
            device_id_type=MESH,
        )

    sends_grad = (None, None, c >= 4, down)
    gets_grad = (None, None, down & up, up)

    def out_copy(kind, j):
        return pltpu.make_async_remote_copy(
            src_ref=(produced, dx)[kind].at[j],
            dst_ref=(next_ref, up_ref)[kind].at[:, columns(j)],
            send_sem=out_send.at[kind, j],
            recv_sem=out_recv.at[kind, j],
            device_id={"pipe": (after, before)[kind]},
            device_id_type=MESH,
        )

    def digit_of(stage):
        axis, stride, factor = stages[stage]
        return lax.rem(lax.axis_index(axis) // stride, factor)

    def sum_peer(stage, offset):
        axis, stride, factor = stages[stage]
        digit = digit_of(stage)
        return {axis: lax.axis_index(axis) + (lax.rem(digit + offset, factor) - digit) * stride}

    def sum_copy(stage, offset, sender):
        return pltpu.make_async_remote_copy(
            src_ref=sums.at[stage, digit_of(stage)],
            dst_ref=sums.at[stage, sender],
            send_sem=sum_send.at[stage, offset - 1],
            recv_sem=sum_recv.at[stage, offset - 1],
            device_id=sum_peer(stage, offset),
            device_id_type=MESH,
        )

    def start_sum(stage):
        for offset in range(1, stages[stage][2]):
            sum_copy(stage, offset, digit_of(stage)).start()

    def finish_sum(stage):
        factor = stages[stage][2]
        for offset in range(1, factor):
            sender = lax.rem(digit_of(stage) + factor - offset, factor)
            sum_copy(stage, offset, sender).wait_recv()
        total = sums[stage, 0]
        for digit in range(1, factor):
            total = total + sums[stage, digit]
        if stage + 1 < len(stages):
            sums[stage + 1, digit_of(stage + 1)] = total
            start_sum(stage + 1)
        else:
            total_ref[...] = total * (1.0 / TOK)

    def when(condition, action):
        if condition is None:
            action()
        else:
            pl.when(condition)(action)

    def start_key(t, kind, j, extra=None):
        condition = sends_key[kind]
        if extra is not None:
            condition = condition & extra
        when(condition, lambda: key_copy(t, kind, j).start())

    def wait_key(t, kind, j):
        when(gets_key[kind], lambda: key_copy(t, kind, j).wait_recv())

    def each(action):
        @pl.loop(0, CHUNKS)
        def _(j):
            action(j)

    each(lambda j: load(0, j).start())
    barrier = pltpu.get_barrier_semaphore()

    def greet(device):
        pl.semaphore_signal(barrier, inc=1, device_id=device, device_id_type=MESH)

    greet({"ctx": partner})
    greet({"pipe": after})
    count = 2
    if sizes["pipe"] > 2:
        greet({"pipe": before})
        count += 1
    pl.when(up)(lambda: greet({"ctx": c + 2}))
    pl.when(down)(lambda: greet({"ctx": c - 2}))
    for stage, (axis, stride, factor) in enumerate(stages):
        if axis == "ctx" and factor == 2 and stride <= 2:
            continue
        for offset in range(1, factor):
            greet(sum_peer(stage, offset))
            count += 1
    each(lambda j: load(1, j).start())
    each(lambda j: load(2, j).start())
    pl.semaphore_wait(barrier, count + up.astype(jnp.int32) + down.astype(jnp.int32))

    def first_saved(j):
        load(0, j).wait()
        start_key(0, A, j)
        start_key(0, C, j, even)

    each(first_saved)

    for which in range(2):
        lap = plan_ref[0, which]
        gains[pl.ds(3 * which, 2), :] = jnp.where(lap == 1, norm_ref[1], norm_ref[0])
        gains[pl.ds(3 * which + 2, 1), :] = jnp.where(lap == 1, outg_ref[1], outg_ref[0])
    distance = (
        lax.broadcasted_iota(jnp.int32, (SPAN, TOK), 1)
        + WINDOW
        - lax.broadcasted_iota(jnp.int32, (SPAN, TOK), 0)
    )
    for t, positions in ((0, sav_pos), (1, sec_pos)):
        allowed = (distance >= 0) & (distance < WINDOW) & (distance <= positions[...])
        masks[t] = jnp.where(allowed, 1.0, 0.0).astype(F32)
    for reach in range(1, REACH + 1):

        @pl.when(c < reach)
        def _():
            @pl.loop(0, CHUNKS)
            def _(j):
                for t in range(2):
                    keys[t, j, rows(slot(reach))] = jnp.zeros((TOK, WIDTH), BF16)

    def relay(t, j):
        wait_key(t, A, j)
        start_key(t, B, j)
        start_key(t, C, j, odd == 1)
        start_key(t, D, j, even)

    def relay_last(t, j):
        wait_key(t, B, j)
        start_key(t, D, j, odd == 1)

    each(lambda j: relay(0, j))

    def second(j):
        relay_last(0, j)
        load(1, j).wait()
        start_key(1, A, j)
        start_key(1, C, j, even)

    each(second)

    def normed(x):
        wide = x.astype(F32)
        inverse = lax.rsqrt(jnp.mean(wide * wide, axis=-1, keepdims=True) + EPSILON)
        return wide * inverse, inverse

    def lanes_of(h):
        return pl.ds(pl.multiple_of(h * HEAD_DIM, HEAD_DIM), HEAD_DIM)

    def weights(t, n_all, a, b):
        k = (n_all * b).astype(BF16)
        q = (n_all[WINDOW:] * a).astype(BF16)
        w = jnp.exp(dot(k, q, 1, 1) * SCALE) * masks[t]
        prob = w * (1.0 / jnp.sum(w, axis=0, keepdims=True))
        return q, k, prob

    sum_slot = digit_of(0)

    def backward(j):
        @pl.loop(0, CHUNK_HEADS)
        def _(i):
            lanes = lanes_of(i)
            head = j * CHUNK_HEADS + i
            wide = lanes_of(head)
            a, b, g = (gains[pl.ds(3 + m, 1), wide] for m in range(3))
            x = keys[0, j, :, lanes]
            n_all, inverse = normed(x)
            q, k, prob = weights(0, n_all, a, b)
            p = prob.astype(BF16)
            ct = cot[j, :, lanes].astype(F32)
            d_mix = (ct * g).astype(BF16)
            d_prob = dot(x, d_mix, 1, 1)
            delta = jnp.sum(prob * d_prob, axis=0, keepdims=True)
            d_score = (prob * (d_prob - delta)).astype(BF16)
            mix = dot(p, x, 0, 0)
            d_k = dot(d_score, q, 1, 0)
            d_q = dot(d_score, k, 0, 0)
            d_value = dot(p, d_mix, 1, 0)
            n_own = n_all[WINDOW:]
            d_n = d_k * (b * SCALE)
            d_n_own = d_n[WINDOW:] + d_q * (a * SCALE)

            def through_norm(d, value, scale):
                return scale * (d - value * jnp.mean(d * value, axis=-1, keepdims=True))

            grads[j, :, lanes] = (
                d_value[:WINDOW] + through_norm(d_n[:WINDOW], n_all[:WINDOW], inverse[:WINDOW])
            ).astype(BF16)
            own[j, :, lanes] = d_value[WINDOW:] + through_norm(d_n_own, n_own, inverse[WINDOW:]) + ct
            parts = (
                jnp.sum(d_q * n_own, axis=0, keepdims=True) * SCALE,
                jnp.sum(d_k * n_all, axis=0, keepdims=True) * SCALE,
                jnp.sum(ct * mix, axis=0, keepdims=True),
            )
            for m in range(3):
                sums[0, sum_slot, pl.ds(m * HEADS + head, 1), :] = parts[m]

    def forward(j):
        @pl.loop(0, CHUNK_HEADS)
        def _(i):
            lanes = lanes_of(i)
            wide = lanes_of(j * CHUNK_HEADS + i)
            a, b, g = (gains[pl.ds(m, 1), wide] for m in range(3))
            x = keys[1, j, :, lanes]
            n_all, _ = normed(x)
            _, _, prob = weights(1, n_all, a, b)
            mix = dot(prob.astype(BF16), x, 0, 0)
            produced[j, :, lanes] = (x[WINDOW:].astype(F32) + g * mix).astype(BF16)

    def send_far(j):
        grad_copy(0, j).wait_recv()
        grad_copy(1, j).wait_recv()

        @pl.when(odd == 1)
        def _():
            total = grads[j, rows(slot(4))].astype(F32) + from_partner[1, j].astype(F32)
            grads[j, rows(slot(4))] = total.astype(BF16)

        pl.when(sends_grad[2])(lambda: grad_copy(2, j).start())

    def send_near(j):
        near = grads[j, rows(slot(2))].astype(F32) + from_partner[1 - odd, j].astype(F32)

        @pl.when(gets_grad[2])
        def _():
            grad_copy(2, j).wait_recv()
            grads[j, rows(slot(2))] = (near + from_z4[j].astype(F32)).astype(BF16)

        @pl.when(jnp.logical_not(gets_grad[2]))
        def _():
            grads[j, rows(slot(2))] = near.astype(BF16)

        pl.when(sends_grad[3])(lambda: grad_copy(3, j).start())

    def send_dx(j):
        @pl.when(even)
        def _():
            own[j] = own[j] + from_partner[0, j].astype(F32)

        @pl.when(gets_grad[3])
        def _():
            grad_copy(3, j).wait_recv()
            own[j] = own[j] + from_z2[j].astype(F32)

        dx[j] = own[j].astype(BF16)
        out_copy(1, j).start()

    def middle(j):
        wait_key(0, C, j)
        wait_key(0, D, j)
        load(2, j).wait()
        backward(j)
        grad_copy(0, j).start()
        grad_copy(1, j).start()
        relay(1, j)
        pl.when(j > 0)(lambda: send_far(jnp.maximum(j - 1, 0)))

    each(middle)
    if stages:
        start_sum(0)
    send_far(CHUNKS - 1)
    each(lambda j: relay_last(1, j))
    each(send_near)
    if stages:
        finish_sum(0)

    def last(j):
        wait_key(1, C, j)
        wait_key(1, D, j)
        forward(j)
        out_copy(0, j).start()

    each(last)
    for stage in range(1, len(stages)):
        finish_sum(stage)
    each(send_dx)

    def drain(j):
        for t in range(2):
            for kind in range(4):
                when(sends_key[kind], lambda: key_copy(t, kind, j).wait_send())
        for kind in range(4):
            when(sends_grad[kind], lambda: grad_copy(kind, j).wait_send())
        for kind in range(2):
            out_copy(kind, j).wait_send()
            out_copy(kind, j).wait_recv()

    each(drain)
    for stage, (_, _, factor) in enumerate(stages):
        for offset in range(1, factor):
            sum_copy(stage, offset, digit_of(stage)).wait_send()


def local(
    sizes,
    section_input,
    section_positions,
    saved_input,
    saved_positions,
    cotangent,
    norm_gains,
    output_gains,
    plan,
):
    stages = sum_stages(sizes)
    widest = max([factor for _, _, factor in stages] + [2])
    depth = max(len(stages), 1)
    in_hbm = pl.BlockSpec(memory_space=pl.ANY)
    in_vmem = pl.BlockSpec(memory_space=pltpu.VMEM)
    block = (CHUNKS, TOK, WIDTH)
    produced, grads, totals = pl.pallas_call(
        functools.partial(kernel, sizes),
        out_shape=(
            jax.ShapeDtypeStruct((TOK, FEATURES), BF16),
            jax.ShapeDtypeStruct((TOK, FEATURES), BF16),
            jax.ShapeDtypeStruct((3 * HEADS, HEAD_DIM), F32),
        ),
        in_specs=[
            in_hbm,
            in_vmem,
            in_hbm,
            in_vmem,
            in_hbm,
            in_vmem,
            in_vmem,
            pl.BlockSpec(memory_space=pltpu.SMEM),
        ],
        out_specs=(in_hbm, in_hbm, in_vmem),
        scratch_shapes=[
            pltpu.VMEM((2, CHUNKS, SPAN, WIDTH), BF16),
            pltpu.VMEM(block, BF16),
            pltpu.VMEM((8, FEATURES), F32),
            pltpu.VMEM((2, SPAN, TOK), F32),
            pltpu.VMEM((CHUNKS, WINDOW, WIDTH), BF16),
            pltpu.VMEM(block, F32),
            pltpu.VMEM((2,) + block, BF16),
            pltpu.VMEM(block, BF16),
            pltpu.VMEM(block, BF16),
            pltpu.VMEM(block, BF16),
            pltpu.VMEM(block, BF16),
            pltpu.VMEM((depth, widest, 3 * HEADS, HEAD_DIM), F32),
            pltpu.SemaphoreType.DMA((3, CHUNKS)),
            pltpu.SemaphoreType.DMA((2, 4, CHUNKS)),
            pltpu.SemaphoreType.DMA((2, 4, CHUNKS)),
            pltpu.SemaphoreType.DMA((4, CHUNKS)),
            pltpu.SemaphoreType.DMA((4, CHUNKS)),
            pltpu.SemaphoreType.DMA((2, CHUNKS)),
            pltpu.SemaphoreType.DMA((2, CHUNKS)),
            pltpu.SemaphoreType.DMA((depth, widest)),
            pltpu.SemaphoreType.DMA((depth, widest)),
        ],
        compiler_params=pltpu.CompilerParams(
            collective_id=0, has_side_effects=True, vmem_limit_bytes=40 * 1024 * 1024
        ),
        cost_estimate=pl.CostEstimate(
            flops=9 * 2 * TOK * SPAN * FEATURES,
            bytes_accessed=5 * TOK * FEATURES * 2,
            transcendentals=2 * HEADS * TOK * SPAN,
        ),
    )(
        section_input[0, 0],
        section_positions[0],
        saved_input[0, 0],
        saved_positions[0],
        cotangent[0, 0],
        norm_gains[:, 0],
        output_gains,
        plan[0],
    )
    return (produced[None, None], grads[None, None], totals.reshape(1, 3, FEATURES))


def solution(mesh):
    placed = (
        P("dp", "pipe", "ctx", None),
        P("dp", "pipe", "ctx"),
        P("dp", "pipe", "ctx", None),
        P("dp", "pipe", "ctx"),
        P("dp", "pipe", "ctx", None),
        P(None, "pipe", None, None),
        P(None, "pipe", None),
        P("dp", "pipe", None),
    )
    return jax.shard_map(
        functools.partial(local, {axis: mesh.shape[axis] for axis in ("dp", "pipe", "ctx")}),
        mesh=mesh,
        in_specs=placed,
        out_specs=(
            P("dp", "pipe", "ctx", None),
            P("dp", "pipe", "ctx", None),
            P("pipe", None, None),
        ),
        check_vma=False,
    )
```

```python
import functools

import jax
import jax.numpy as jnp
from jax import lax
from jax.experimental import pallas as pl
from jax.experimental.pallas import tpu as pltpu
from jax.sharding import PartitionSpec as P

HEADS = 16
HEAD_DIM = 128
FEATURES = 2048
WINDOW = 512
TOK = 128
REACH = WINDOW // TOK
SPAN = WINDOW + TOK
CHUNKS = 4
WIDTH = FEATURES // CHUNKS
CHUNK_HEADS = HEADS // CHUNKS
EPSILON = 1e-06
SCALE = HEAD_DIM**-0.5
MESH = pl.DeviceIdType.MESH
F32 = jnp.float32
BF16 = jnp.bfloat16
A, B, C, D = range(4)
LAST = CHUNKS - 1


def sum_stages(sizes):
    stages = []
    for axis in ("dp", "ctx"):
        left, stride = sizes[axis], 1
        while left > 1:
            factor = next(f for f in range(2, left + 1) if left % f == 0)
            stages.append((axis, stride, factor))
            left //= factor
            stride *= factor
    return stages


def slot(reach):
    return (REACH - reach) * TOK


def dot(left, right, left_dim, right_dim):
    return lax.dot_general(
        left, right, (((left_dim,), (right_dim,)), ((), ())), preferred_element_type=F32
    )


def kernel(
    sizes,
    sec_ref,
    sec_pos,
    sav_ref,
    sav_pos,
    cot_ref,
    norm_ref,
    outg_ref,
    plan_ref,
    next_ref,
    up_ref,
    total_ref,
    keys,
    cot,
    gains,
    masks,
    grads,
    own,
    from_partner,
    from_z3,
    from_z4,
    from_z2,
    produced,
    dx,
    sums,
    load_sem,
    key_send,
    key_recv,
    grad_send,
    grad_recv,
    out_send,
    out_recv,
    sum_send,
    sum_recv,
):
    n = sizes["ctx"]
    c = lax.axis_index("ctx")
    odd = lax.rem(c, 2)
    even = odd == 0
    partner = c + 1 - 2 * odd
    pipe = lax.axis_index("pipe")
    after = lax.rem(pipe + 1, sizes["pipe"])
    before = lax.rem(pipe + sizes["pipe"] - 1, sizes["pipe"])
    up, down = c + 2 < n, c >= 2
    stages = sum_stages(sizes)

    def rows(first):
        if isinstance(first, int):
            return pl.ds(first, TOK)
        return pl.ds(pl.multiple_of(first, TOK), TOK)

    def columns(j):
        return pl.ds(pl.multiple_of(j * WIDTH, WIDTH), WIDTH)

    def load(which, j):
        source = (sav_ref, sec_ref, cot_ref)[which]
        target = cot.at[j] if which == 2 else keys.at[which, j, rows(WINDOW)]
        return pltpu.make_async_copy(source.at[:, columns(j)], target, load_sem.at[which, j])

    def key_copy(t, kind, j):
        if kind == A:
            source, target, device = slot(0), slot(2), c + 2
        elif kind == B:
            source, target, device = slot(2), slot(4), c + 2
        elif kind == C:
            source, target, device = jnp.where(even, slot(0), slot(2)), slot(1), partner
        else:
            source = jnp.where(j == LAST, slot(1), jnp.where(even, slot(2), slot(4)))
            target, device = slot(3), jnp.where(j == LAST, c + 2, partner)
        return pltpu.make_async_remote_copy(
            src_ref=keys.at[t, j, rows(source)],
            dst_ref=keys.at[t, j, rows(target)],
            send_sem=key_send.at[t, kind, j],
            recv_sem=key_recv.at[t, kind, j],
            device_id={"ctx": device},
            device_id_type=MESH,
        )

    def sends_key(kind, j):
        if kind == D:
            return ((j == LAST) & up & (c >= 1)) | ((j < LAST) & (c >= 2 + 2 * odd))
        return (up, up & down, even | down)[kind]

    gets_key = (c >= 2, c >= 4, c >= 1, c >= 3)

    def grad_copy(kind, j):
        first = slot((3, 4, 1, 2)[kind])
        target = (from_z3, from_z4, from_partner, from_z2)[kind].at[j]
        return pltpu.make_async_remote_copy(
            src_ref=grads.at[j, rows(first)],
            dst_ref=target,
            send_sem=grad_send.at[kind, j],
            recv_sem=grad_recv.at[kind, j],
            device_id={"ctx": partner if kind == 2 else c - 2},
            device_id_type=MESH,
        )

    sends_grad = (down, down, None, down)

    def out_copy(kind, j):
        return pltpu.make_async_remote_copy(
            src_ref=(produced, dx)[kind].at[j],
            dst_ref=(next_ref, up_ref)[kind].at[:, columns(j)],
            send_sem=out_send.at[kind, j],
            recv_sem=out_recv.at[kind, j],
            device_id={"pipe": (after, before)[kind]},
            device_id_type=MESH,
        )

    def digit_of(stage):
        axis, stride, factor = stages[stage]
        return lax.rem(lax.axis_index(axis) // stride, factor)

    def sum_peer(stage, offset):
        axis, stride, factor = stages[stage]
        digit = digit_of(stage)
        return {axis: lax.axis_index(axis) + (lax.rem(digit + offset, factor) - digit) * stride}

    def sum_copy(stage, offset, sender):
        return pltpu.make_async_remote_copy(
            src_ref=sums.at[stage, digit_of(stage)],
            dst_ref=sums.at[stage, sender],
            send_sem=sum_send.at[stage, offset - 1],
            recv_sem=sum_recv.at[stage, offset - 1],
            device_id=sum_peer(stage, offset),
            device_id_type=MESH,
        )

    def start_sum(stage):
        for offset in range(1, stages[stage][2]):
            sum_copy(stage, offset, digit_of(stage)).start()

    def finish_sum(stage):
        factor = stages[stage][2]
        for offset in range(1, factor):
            sender = lax.rem(digit_of(stage) + factor - offset, factor)
            sum_copy(stage, offset, sender).wait_recv()
        total = sums[stage, 0]
        for digit in range(1, factor):
            total = total + sums[stage, digit]
        if stage + 1 < len(stages):
            sums[stage + 1, digit_of(stage + 1)] = total
            start_sum(stage + 1)
        else:
            total_ref[...] = total * (1.0 / TOK)

    def when(condition, action):
        if condition is None:
            action()
        else:
            pl.when(condition)(action)

    def start_key(t, kind, j, extra=None):
        condition = sends_key(kind, j)
        if extra is not None:
            condition = condition & extra
        when(condition, lambda: key_copy(t, kind, j).start())

    def wait_key(t, kind, j, extra=None):
        condition = gets_key[kind]
        if extra is not None:
            condition = condition & extra
        when(condition, lambda: key_copy(t, kind, j).wait_recv())

    def each(action):
        @pl.loop(0, CHUNKS)
        def _(j):
            action(j)

    each(lambda j: load(0, j).start())
    barrier = pltpu.get_barrier_semaphore()

    def greet(device):
        pl.semaphore_signal(barrier, inc=1, device_id=device, device_id_type=MESH)

    greet({"ctx": partner})
    greet({"pipe": after})
    count = 2
    if sizes["pipe"] > 2:
        greet({"pipe": before})
        count += 1
    pl.when(up)(lambda: greet({"ctx": c + 2}))
    pl.when(down)(lambda: greet({"ctx": c - 2}))
    for stage, (axis, stride, factor) in enumerate(stages):
        if axis == "ctx" and factor == 2 and stride <= 2:
            continue
        for offset in range(1, factor):
            greet(sum_peer(stage, offset))
            count += 1
    each(lambda j: load(1, j).start())
    each(lambda j: load(2, j).start())
    pl.semaphore_wait(barrier, count + up.astype(jnp.int32) + down.astype(jnp.int32))

    def first_saved(j):
        load(0, j).wait()
        start_key(0, A, j)
        start_key(0, C, j, even)

    each(first_saved)

    for which in range(2):
        lap = plan_ref[0, which]
        gains[pl.ds(3 * which, 2), :] = jnp.where(lap == 1, norm_ref[1], norm_ref[0])
        gains[pl.ds(3 * which + 2, 1), :] = jnp.where(lap == 1, outg_ref[1], outg_ref[0])
    distance = (
        lax.broadcasted_iota(jnp.int32, (SPAN, TOK), 1)
        + WINDOW
        - lax.broadcasted_iota(jnp.int32, (SPAN, TOK), 0)
    )
    for t, positions in ((0, sav_pos), (1, sec_pos)):
        allowed = (distance >= 0) & (distance < WINDOW) & (distance <= positions[...])
        masks[t] = jnp.where(allowed, 1.0, 0.0).astype(F32)
    for reach in range(1, REACH + 1):

        @pl.when(c < reach)
        def _():
            @pl.loop(0, CHUNKS)
            def _(j):
                for t in range(2):
                    keys[t, j, rows(slot(reach))] = jnp.zeros((TOK, WIDTH), BF16)

    def relay(t, j):
        wait_key(t, A, j)
        start_key(t, B, j)
        start_key(t, C, j, odd == 1)
        start_key(t, D, j, even & (j < LAST))

    def relay_last(t, j):
        wait_key(t, B, j)
        wait_key(t, C, j, j == LAST)
        start_key(t, D, j, (odd == 1) | (j == LAST))

    each(lambda j: relay(0, j))

    def second(j):
        relay_last(0, j)
        load(1, j).wait()
        start_key(1, A, j)
        start_key(1, C, j, even)

    each(second)

    def normed(x):
        wide = x.astype(F32)
        inverse = lax.rsqrt(jnp.mean(wide * wide, axis=-1, keepdims=True) + EPSILON)
        return wide * inverse, inverse

    def lanes_of(h):
        return pl.ds(pl.multiple_of(h * HEAD_DIM, HEAD_DIM), HEAD_DIM)

    def weights(t, n_all, a, b):
        k = (n_all * b).astype(BF16)
        q = (n_all[WINDOW:] * a).astype(BF16)
        w = jnp.exp(dot(k, q, 1, 1) * SCALE) * masks[t]
        prob = w * (1.0 / jnp.sum(w, axis=0, keepdims=True))
        return q, k, prob

    sum_slot = digit_of(0)

    def backward(j):
        @pl.loop(0, CHUNK_HEADS)
        def _(i):
            lanes = lanes_of(i)
            head = j * CHUNK_HEADS + i
            wide = lanes_of(head)
            a, b, g = (gains[pl.ds(3 + m, 1), wide] for m in range(3))
            x = keys[0, j, :, lanes]
            n_all, inverse = normed(x)
            q, k, prob = weights(0, n_all, a, b)
            p = prob.astype(BF16)
            ct = cot[j, :, lanes].astype(F32)
            d_mix = (ct * g).astype(BF16)
            d_prob = dot(x, d_mix, 1, 1)
            delta = jnp.sum(prob * d_prob, axis=0, keepdims=True)
            d_score = (prob * (d_prob - delta)).astype(BF16)
            mix = dot(p, x, 0, 0)
            d_k = dot(d_score, q, 1, 0)
            d_q = dot(d_score, k, 0, 0)
            d_value = dot(p, d_mix, 1, 0)
            n_own = n_all[WINDOW:]
            d_n = d_k * (b * SCALE)
            d_n_own = d_n[WINDOW:] + d_q * (a * SCALE)

            def through_norm(d, value, scale):
                return scale * (d - value * jnp.mean(d * value, axis=-1, keepdims=True))

            grads[j, :, lanes] = (
                d_value[:WINDOW] + through_norm(d_n[:WINDOW], n_all[:WINDOW], inverse[:WINDOW])
            ).astype(BF16)
            own[j, :, lanes] = d_value[WINDOW:] + through_norm(d_n_own, n_own, inverse[WINDOW:]) + ct
            parts = (
                jnp.sum(d_q * n_own, axis=0, keepdims=True) * SCALE,
                jnp.sum(d_k * n_all, axis=0, keepdims=True) * SCALE,
                jnp.sum(ct * mix, axis=0, keepdims=True),
            )
            for m in range(3):
                sums[0, sum_slot, pl.ds(m * HEADS + head, 1), :] = parts[m]

    def forward(j):
        @pl.loop(0, CHUNK_HEADS)
        def _(i):
            lanes = lanes_of(i)
            wide = lanes_of(j * CHUNK_HEADS + i)
            a, b, g = (gains[pl.ds(m, 1), wide] for m in range(3))
            x = keys[1, j, :, lanes]
            n_all, _ = normed(x)
            _, _, prob = weights(1, n_all, a, b)
            mix = dot(prob.astype(BF16), x, 0, 0)
            produced[j, :, lanes] = (x[WINDOW:].astype(F32) + g * mix).astype(BF16)

    def add_to(reach, j, received):
        total = grads[j, rows(slot(reach))].astype(F32) + received[j].astype(F32)
        grads[j, rows(slot(reach))] = total.astype(BF16)

    def merge(j):
        @pl.when(up)
        def _():
            grad_copy(0, j).wait_recv()
            add_to(1, j, from_z3)

        grad_copy(2, j).start()

        @pl.when(up)
        def _():
            grad_copy(1, j).wait_recv()
            add_to(2, j, from_z4)

        pl.when(even & down)(lambda: grad_copy(3, j).start())

    def pass_on(j):
        @pl.when(odd == 1)
        def _():
            grad_copy(2, j).wait_recv()
            add_to(2, j, from_partner)
            pl.when(down)(lambda: grad_copy(3, j).start())

    def send_dx(j):
        @pl.when(even)
        def _():
            grad_copy(2, j).wait_recv()
            own[j] = own[j] + from_partner[j].astype(F32)

        @pl.when(up)
        def _():
            grad_copy(3, j).wait_recv()
            own[j] = own[j] + from_z2[j].astype(F32)

        dx[j] = own[j].astype(BF16)
        out_copy(1, j).start()

    def middle(j):
        wait_key(0, C, j, j < LAST)
        wait_key(0, D, j)
        pl.when(j == 0)(lambda: each(lambda i: load(2, i).wait()))
        backward(j)
        for kind in range(2):
            when(sends_grad[kind], lambda: grad_copy(kind, j).start())
        relay(1, j)
        pl.when(j > 0)(lambda: merge(jnp.maximum(j - 1, 0)))

    each(middle)
    if stages:
        start_sum(0)
    merge(LAST)

    def between(j):
        pass_on(j)
        relay_last(1, j)

    each(between)
    if stages:
        finish_sum(0)

    def last(j):
        wait_key(1, C, j, j < LAST)
        wait_key(1, D, j)
        forward(j)
        out_copy(0, j).start()
        for stage in range(1, min(CHUNKS + 1, len(stages))):
            pl.when(j == stage - 1)(lambda: finish_sum(stage))
        send_dx(j)

    each(last)
    for stage in range(CHUNKS + 1, len(stages)):
        finish_sum(stage)

    def drain(j):
        for t in range(2):
            for kind in range(4):
                when(sends_key(kind, j), lambda: key_copy(t, kind, j).wait_send())
        for kind in range(4):
            when(sends_grad[kind], lambda: grad_copy(kind, j).wait_send())
        for kind in range(2):
            out_copy(kind, j).wait_send()
            out_copy(kind, j).wait_recv()

    each(drain)
    for stage, (_, _, factor) in enumerate(stages):
        for offset in range(1, factor):
            sum_copy(stage, offset, digit_of(stage)).wait_send()


def local(
    sizes,
    section_input,
    section_positions,
    saved_input,
    saved_positions,
    cotangent,
    norm_gains,
    output_gains,
    plan,
):
    stages = sum_stages(sizes)
    widest = max([factor for _, _, factor in stages] + [2])
    depth = max(len(stages), 1)
    in_hbm = pl.BlockSpec(memory_space=pl.ANY)
    in_vmem = pl.BlockSpec(memory_space=pltpu.VMEM)
    block = (CHUNKS, TOK, WIDTH)
    produced, grads, totals = pl.pallas_call(
        functools.partial(kernel, sizes),
        out_shape=(
            jax.ShapeDtypeStruct((TOK, FEATURES), BF16),
            jax.ShapeDtypeStruct((TOK, FEATURES), BF16),
            jax.ShapeDtypeStruct((3 * HEADS, HEAD_DIM), F32),
        ),
        in_specs=[
            in_hbm,
            in_vmem,
            in_hbm,
            in_vmem,
            in_hbm,
            in_vmem,
            in_vmem,
            pl.BlockSpec(memory_space=pltpu.SMEM),
        ],
        out_specs=(in_hbm, in_hbm, in_vmem),
        scratch_shapes=[
            pltpu.VMEM((2, CHUNKS, SPAN, WIDTH), BF16),
            pltpu.VMEM(block, BF16),
            pltpu.VMEM((8, FEATURES), F32),
            pltpu.VMEM((2, SPAN, TOK), F32),
            pltpu.VMEM((CHUNKS, WINDOW, WIDTH), BF16),
            pltpu.VMEM(block, F32),
            pltpu.VMEM(block, BF16),
            pltpu.VMEM(block, BF16),
            pltpu.VMEM(block, BF16),
            pltpu.VMEM(block, BF16),
            pltpu.VMEM(block, BF16),
            pltpu.VMEM(block, BF16),
            pltpu.VMEM((depth, widest, 3 * HEADS, HEAD_DIM), F32),
            pltpu.SemaphoreType.DMA((3, CHUNKS)),
            pltpu.SemaphoreType.DMA((2, 4, CHUNKS)),
            pltpu.SemaphoreType.DMA((2, 4, CHUNKS)),
            pltpu.SemaphoreType.DMA((4, CHUNKS)),
            pltpu.SemaphoreType.DMA((4, CHUNKS)),
            pltpu.SemaphoreType.DMA((2, CHUNKS)),
            pltpu.SemaphoreType.DMA((2, CHUNKS)),
            pltpu.SemaphoreType.DMA((depth, widest)),
            pltpu.SemaphoreType.DMA((depth, widest)),
        ],
        compiler_params=pltpu.CompilerParams(
            collective_id=0, has_side_effects=True, vmem_limit_bytes=60 * 1024 * 1024
        ),
        cost_estimate=pl.CostEstimate(
            flops=9 * 2 * TOK * SPAN * FEATURES,
            bytes_accessed=5 * TOK * FEATURES * 2,
            transcendentals=2 * HEADS * TOK * SPAN,
        ),
    )(
        section_input[0, 0],
        section_positions[0],
        saved_input[0, 0],
        saved_positions[0],
        cotangent[0, 0],
        norm_gains[:, 0],
        output_gains,
        plan[0],
    )
    return (produced[None, None], grads[None, None], totals.reshape(1, 3, FEATURES))


def solution(mesh):
    placed = (
        P("dp", "pipe", "ctx", None),
        P("dp", "pipe", "ctx"),
        P("dp", "pipe", "ctx", None),
        P("dp", "pipe", "ctx"),
        P("dp", "pipe", "ctx", None),
        P(None, "pipe", None, None),
        P(None, "pipe", None),
        P("dp", "pipe", None),
    )
    return jax.shard_map(
        functools.partial(local, {axis: mesh.shape[axis] for axis in ("dp", "pipe", "ctx")}),
        mesh=mesh,
        in_specs=placed,
        out_specs=(
            P("dp", "pipe", "ctx", None),
            P("dp", "pipe", "ctx", None),
            P("pipe", None, None),
        ),
        check_vma=False,
    )
```

```python
import functools

import jax
import jax.numpy as jnp
from jax import lax
from jax.experimental import pallas as pl
from jax.experimental.pallas import tpu as pltpu
from jax.sharding import PartitionSpec as P

HEADS = 16
HEAD_DIM = 128
FEATURES = 2048
WINDOW = 512
TOK = 128
REACH = WINDOW // TOK
SPAN = WINDOW + TOK
CHUNKS = 4
WIDTH = FEATURES // CHUNKS
CHUNK_HEADS = HEADS // CHUNKS
EPSILON = 1e-06
SCALE = HEAD_DIM**-0.5
MESH = pl.DeviceIdType.MESH
F32 = jnp.float32
BF16 = jnp.bfloat16
A, B, C, D = range(4)
LAST = CHUNKS - 1


def sum_stages(sizes):
    stages = []
    for axis in ("dp", "ctx"):
        left, stride = sizes[axis], 1
        while left > 1:
            factor = next(f for f in range(2, left + 1) if left % f == 0)
            stages.append((axis, stride, factor))
            left //= factor
            stride *= factor
    return stages


def slot(reach):
    return (REACH - reach) * TOK


def dot(left, right, left_dim, right_dim):
    return lax.dot_general(
        left, right, (((left_dim,), (right_dim,)), ((), ())), preferred_element_type=F32
    )


def kernel(
    sizes,
    sec_ref,
    sec_pos,
    sav_ref,
    sav_pos,
    cot_ref,
    norm_ref,
    outg_ref,
    plan_ref,
    next_ref,
    up_ref,
    total_ref,
    keys,
    cot,
    gains,
    masks,
    grads,
    own,
    from_partner,
    from_z3,
    from_z4,
    from_z2,
    produced,
    dx,
    sums,
    load_sem,
    key_send,
    key_recv,
    grad_send,
    grad_recv,
    out_send,
    out_recv,
    sum_send,
    sum_recv,
):
    n = sizes["ctx"]
    c = lax.axis_index("ctx")
    odd = lax.rem(c, 2)
    even = odd == 0
    partner = c + 1 - 2 * odd
    pipe = lax.axis_index("pipe")
    after = lax.rem(pipe + 1, sizes["pipe"])
    before = lax.rem(pipe + sizes["pipe"] - 1, sizes["pipe"])
    up, down = c + 2 < n, c >= 2
    stages = sum_stages(sizes)

    def rows(first):
        if isinstance(first, int):
            return pl.ds(first, TOK)
        return pl.ds(pl.multiple_of(first, TOK), TOK)

    def columns(j):
        return pl.ds(pl.multiple_of(j * WIDTH, WIDTH), WIDTH)

    def load(which, j):
        source = (sav_ref, sec_ref, cot_ref)[which]
        target = cot.at[j] if which == 2 else keys.at[which, j, rows(WINDOW)]
        return pltpu.make_async_copy(source.at[:, columns(j)], target, load_sem.at[which, j])

    def key_copy(t, kind, j):
        if kind == A:
            source, target, device = slot(0), slot(2), c + 2
        elif kind == B:
            source, target, device = slot(2), slot(4), c + 2
        elif kind == C:
            source, target, device = jnp.where(even, slot(0), slot(2)), slot(1), partner
        else:
            source = jnp.where(j == LAST, slot(1), jnp.where(even, slot(2), slot(4)))
            target, device = slot(3), jnp.where(j == LAST, c + 2, partner)
        return pltpu.make_async_remote_copy(
            src_ref=keys.at[t, j, rows(source)],
            dst_ref=keys.at[t, j, rows(target)],
            send_sem=key_send.at[t, kind, j],
            recv_sem=key_recv.at[t, kind, j],
            device_id={"ctx": device},
            device_id_type=MESH,
        )

    def sends_key(kind, j):
        if kind == D:
            return ((j == LAST) & up & (c >= 1)) | ((j < LAST) & (c >= 2 + 2 * odd))
        return (up, up & down, even | down)[kind]

    gets_key = (c >= 2, c >= 4, c >= 1, c >= 3)

    def grad_copy(kind, j):
        first = slot((3, 4, 1, 2)[kind])
        target = (from_z3, from_z4, from_partner, from_z2)[kind].at[j]
        return pltpu.make_async_remote_copy(
            src_ref=grads.at[j, rows(first)],
            dst_ref=target,
            send_sem=grad_send.at[kind, j],
            recv_sem=grad_recv.at[kind, j],
            device_id={"ctx": partner if kind == 2 else c - 2},
            device_id_type=MESH,
        )

    sends_grad = (down, down, None, down)

    def out_copy(kind, j):
        return pltpu.make_async_remote_copy(
            src_ref=(produced, dx)[kind].at[j],
            dst_ref=(next_ref, up_ref)[kind].at[:, columns(j)],
            send_sem=out_send.at[kind, j],
            recv_sem=out_recv.at[kind, j],
            device_id={"pipe": (after, before)[kind]},
            device_id_type=MESH,
        )

    def digit_of(stage):
        axis, stride, factor = stages[stage]
        return lax.rem(lax.axis_index(axis) // stride, factor)

    def sum_peer(stage, offset):
        axis, stride, factor = stages[stage]
        digit = digit_of(stage)
        return {axis: lax.axis_index(axis) + (lax.rem(digit + offset, factor) - digit) * stride}

    def sum_copy(stage, offset, sender):
        return pltpu.make_async_remote_copy(
            src_ref=sums.at[stage, digit_of(stage)],
            dst_ref=sums.at[stage, sender],
            send_sem=sum_send.at[stage, offset - 1],
            recv_sem=sum_recv.at[stage, offset - 1],
            device_id=sum_peer(stage, offset),
            device_id_type=MESH,
        )

    def start_sum(stage):
        for offset in range(1, stages[stage][2]):
            sum_copy(stage, offset, digit_of(stage)).start()

    def finish_sum(stage):
        factor = stages[stage][2]
        for offset in range(1, factor):
            sender = lax.rem(digit_of(stage) + factor - offset, factor)
            sum_copy(stage, offset, sender).wait_recv()
        total = sums[stage, 0]
        for digit in range(1, factor):
            total = total + sums[stage, digit]
        if stage + 1 < len(stages):
            sums[stage + 1, digit_of(stage + 1)] = total
            start_sum(stage + 1)
        else:
            total_ref[...] = total * (1.0 / TOK)

    def when(condition, action):
        if condition is None:
            action()
        else:
            pl.when(condition)(action)

    def start_key(t, kind, j, extra=None):
        condition = sends_key(kind, j)
        if extra is not None:
            condition = condition & extra
        when(condition, lambda: key_copy(t, kind, j).start())

    def wait_key(t, kind, j, extra=None):
        condition = gets_key[kind]
        if extra is not None:
            condition = condition & extra
        when(condition, lambda: key_copy(t, kind, j).wait_recv())

    def each(action):
        @pl.loop(0, CHUNKS)
        def _(j):
            action(j)

    each(lambda j: load(0, j).start())
    barrier = pltpu.get_barrier_semaphore()

    def greet(device):
        pl.semaphore_signal(barrier, inc=1, device_id=device, device_id_type=MESH)

    greet({"ctx": partner})
    greet({"pipe": after})
    count = 2
    if sizes["pipe"] > 2:
        greet({"pipe": before})
        count += 1
    pl.when(up)(lambda: greet({"ctx": c + 2}))
    pl.when(down)(lambda: greet({"ctx": c - 2}))
    for stage, (axis, stride, factor) in enumerate(stages):
        if axis == "ctx" and factor == 2 and stride <= 2:
            continue
        for offset in range(1, factor):
            greet(sum_peer(stage, offset))
            count += 1
    each(lambda j: load(1, j).start())
    each(lambda j: load(2, j).start())
    pl.semaphore_wait(barrier, count + up.astype(jnp.int32) + down.astype(jnp.int32))

    def first_saved(j):
        load(0, j).wait()
        start_key(0, A, j)
        start_key(0, C, j, even)

    each(first_saved)

    for which in range(2):
        lap = plan_ref[0, which]
        gains[pl.ds(3 * which, 2), :] = jnp.where(lap == 1, norm_ref[1], norm_ref[0])
        gains[pl.ds(3 * which + 2, 1), :] = jnp.where(lap == 1, outg_ref[1], outg_ref[0])
    distance = (
        lax.broadcasted_iota(jnp.int32, (SPAN, TOK), 1)
        + WINDOW
        - lax.broadcasted_iota(jnp.int32, (SPAN, TOK), 0)
    )
    for t, positions in ((0, sav_pos), (1, sec_pos)):
        allowed = (distance >= 0) & (distance < WINDOW) & (distance <= positions[...])
        masks[t] = jnp.where(allowed, 1.0, 0.0).astype(F32)
    for reach in range(1, REACH + 1):

        @pl.when(c < reach)
        def _():
            @pl.loop(0, CHUNKS)
            def _(j):
                for t in range(2):
                    keys[t, j, rows(slot(reach))] = jnp.zeros((TOK, WIDTH), BF16)

    def relay(t, j):
        wait_key(t, A, j)
        start_key(t, B, j)
        start_key(t, C, j, odd == 1)
        start_key(t, D, j, even & (j < LAST))

    def relay_last(t, j):
        wait_key(t, B, j)
        wait_key(t, C, j, j == LAST)
        start_key(t, D, j, (odd == 1) | (j == LAST))

    each(lambda j: relay(0, j))

    def second(j):
        relay_last(0, j)
        load(1, j).wait()
        start_key(1, A, j)
        start_key(1, C, j, even)

    each(second)

    def normed(x):
        wide = x.astype(F32)
        inverse = lax.rsqrt(jnp.mean(wide * wide, axis=-1, keepdims=True) + EPSILON)
        return wide * inverse, inverse

    def lanes_of(h):
        return pl.ds(pl.multiple_of(h * HEAD_DIM, HEAD_DIM), HEAD_DIM)

    def weights(t, n_all, a, b):
        k = (n_all * b).astype(BF16)
        q = (n_all[WINDOW:] * a).astype(BF16)
        w = jnp.exp(dot(k, q, 1, 1) * SCALE) * masks[t]
        prob = w * (1.0 / jnp.sum(w, axis=0, keepdims=True))
        return q, k, prob

    sum_slot = digit_of(0)

    def backward(j):
        @pl.loop(0, CHUNK_HEADS, unroll=4)
        def _(i):
            lanes = lanes_of(i)
            head = j * CHUNK_HEADS + i
            wide = lanes_of(head)
            a, b, g = (gains[pl.ds(3 + m, 1), wide] for m in range(3))
            x = keys[0, j, :, lanes]
            n_all, inverse = normed(x)
            q, k, prob = weights(0, n_all, a, b)
            p = prob.astype(BF16)
            ct = cot[j, :, lanes].astype(F32)
            d_mix = (ct * g).astype(BF16)
            d_prob = dot(x, d_mix, 1, 1)
            delta = jnp.sum(prob * d_prob, axis=0, keepdims=True)
            d_score = (prob * (d_prob - delta)).astype(BF16)
            mix = dot(p, x, 0, 0)
            d_k = dot(d_score, q, 1, 0)
            d_q = dot(d_score, k, 0, 0)
            d_value = dot(p, d_mix, 1, 0)
            n_own = n_all[WINDOW:]
            d_n = d_k * (b * SCALE)
            d_n_own = d_n[WINDOW:] + d_q * (a * SCALE)

            def through_norm(d, value, scale):
                return scale * (d - value * jnp.mean(d * value, axis=-1, keepdims=True))

            grads[j, :, lanes] = (
                d_value[:WINDOW] + through_norm(d_n[:WINDOW], n_all[:WINDOW], inverse[:WINDOW])
            ).astype(BF16)
            own[j, :, lanes] = d_value[WINDOW:] + through_norm(d_n_own, n_own, inverse[WINDOW:]) + ct
            parts = (
                jnp.sum(d_q * n_own, axis=0, keepdims=True) * SCALE,
                jnp.sum(d_k * n_all, axis=0, keepdims=True) * SCALE,
                jnp.sum(ct * mix, axis=0, keepdims=True),
            )
            for m in range(3):
                sums[0, sum_slot, pl.ds(m * HEADS + head, 1), :] = parts[m]

    def forward(j):
        @pl.loop(0, CHUNK_HEADS, unroll=4)
        def _(i):
            lanes = lanes_of(i)
            wide = lanes_of(j * CHUNK_HEADS + i)
            a, b, g = (gains[pl.ds(m, 1), wide] for m in range(3))
            x = keys[1, j, :, lanes]
            n_all, _ = normed(x)
            _, _, prob = weights(1, n_all, a, b)
            mix = dot(prob.astype(BF16), x, 0, 0)
            produced[j, :, lanes] = (x[WINDOW:].astype(F32) + g * mix).astype(BF16)

    def add_to(reach, j, received):
        total = grads[j, rows(slot(reach))].astype(F32) + received[j].astype(F32)
        grads[j, rows(slot(reach))] = total.astype(BF16)

    def merge(j):
        @pl.when(up)
        def _():
            grad_copy(0, j).wait_recv()
            add_to(1, j, from_z3)

        grad_copy(2, j).start()

        @pl.when(up)
        def _():
            grad_copy(1, j).wait_recv()
            add_to(2, j, from_z4)

        pl.when(even & down)(lambda: grad_copy(3, j).start())

    def pass_on(j):
        @pl.when(odd == 1)
        def _():
            grad_copy(2, j).wait_recv()
            add_to(2, j, from_partner)
            pl.when(down)(lambda: grad_copy(3, j).start())

    def send_dx(j):
        @pl.when(even)
        def _():
            grad_copy(2, j).wait_recv()
            own[j] = own[j] + from_partner[j].astype(F32)

        @pl.when(up)
        def _():
            grad_copy(3, j).wait_recv()
            own[j] = own[j] + from_z2[j].astype(F32)

        dx[j] = own[j].astype(BF16)
        out_copy(1, j).start()

    def middle(j):
        wait_key(0, C, j, j < LAST)
        wait_key(0, D, j)
        pl.when(j == 0)(lambda: each(lambda i: load(2, i).wait()))
        backward(j)
        for kind in range(2):
            when(sends_grad[kind], lambda: grad_copy(kind, j).start())
        relay(1, j)
        pl.when(j > 0)(lambda: merge(jnp.maximum(j - 1, 0)))

    each(middle)
    if stages:
        start_sum(0)
    merge(LAST)

    def between(j):
        pass_on(j)
        relay_last(1, j)

    each(between)
    if stages:
        finish_sum(0)

    def last(j):
        wait_key(1, C, j, j < LAST)
        wait_key(1, D, j)
        forward(j)
        out_copy(0, j).start()
        for stage in range(1, min(CHUNKS + 1, len(stages))):
            pl.when(j == stage - 1)(lambda: finish_sum(stage))
        send_dx(j)

    each(last)
    for stage in range(CHUNKS + 1, len(stages)):
        finish_sum(stage)

    def drain(j):
        for t in range(2):
            for kind in range(4):
                when(sends_key(kind, j), lambda: key_copy(t, kind, j).wait_send())
        for kind in range(4):
            when(sends_grad[kind], lambda: grad_copy(kind, j).wait_send())
        for kind in range(2):
            out_copy(kind, j).wait_send()
            out_copy(kind, j).wait_recv()

    each(drain)
    for stage, (_, _, factor) in enumerate(stages):
        for offset in range(1, factor):
            sum_copy(stage, offset, digit_of(stage)).wait_send()


def local(
    sizes,
    section_input,
    section_positions,
    saved_input,
    saved_positions,
    cotangent,
    norm_gains,
    output_gains,
    plan,
):
    stages = sum_stages(sizes)
    widest = max([factor for _, _, factor in stages] + [2])
    depth = max(len(stages), 1)
    in_hbm = pl.BlockSpec(memory_space=pl.ANY)
    in_vmem = pl.BlockSpec(memory_space=pltpu.VMEM)
    block = (CHUNKS, TOK, WIDTH)
    produced, grads, totals = pl.pallas_call(
        functools.partial(kernel, sizes),
        out_shape=(
            jax.ShapeDtypeStruct((TOK, FEATURES), BF16),
            jax.ShapeDtypeStruct((TOK, FEATURES), BF16),
            jax.ShapeDtypeStruct((3 * HEADS, HEAD_DIM), F32),
        ),
        in_specs=[
            in_hbm,
            in_vmem,
            in_hbm,
            in_vmem,
            in_hbm,
            in_vmem,
            in_vmem,
            pl.BlockSpec(memory_space=pltpu.SMEM),
        ],
        out_specs=(in_hbm, in_hbm, in_vmem),
        scratch_shapes=[
            pltpu.VMEM((2, CHUNKS, SPAN, WIDTH), BF16),
            pltpu.VMEM(block, BF16),
            pltpu.VMEM((8, FEATURES), F32),
            pltpu.VMEM((2, SPAN, TOK), F32),
            pltpu.VMEM((CHUNKS, WINDOW, WIDTH), BF16),
            pltpu.VMEM(block, F32),
            pltpu.VMEM(block, BF16),
            pltpu.VMEM(block, BF16),
            pltpu.VMEM(block, BF16),
            pltpu.VMEM(block, BF16),
            pltpu.VMEM(block, BF16),
            pltpu.VMEM(block, BF16),
            pltpu.VMEM((depth, widest, 3 * HEADS, HEAD_DIM), F32),
            pltpu.SemaphoreType.DMA((3, CHUNKS)),
            pltpu.SemaphoreType.DMA((2, 4, CHUNKS)),
            pltpu.SemaphoreType.DMA((2, 4, CHUNKS)),
            pltpu.SemaphoreType.DMA((4, CHUNKS)),
            pltpu.SemaphoreType.DMA((4, CHUNKS)),
            pltpu.SemaphoreType.DMA((2, CHUNKS)),
            pltpu.SemaphoreType.DMA((2, CHUNKS)),
            pltpu.SemaphoreType.DMA((depth, widest)),
            pltpu.SemaphoreType.DMA((depth, widest)),
        ],
        compiler_params=pltpu.CompilerParams(
            collective_id=0, has_side_effects=True, vmem_limit_bytes=60 * 1024 * 1024
        ),
        cost_estimate=pl.CostEstimate(
            flops=9 * 2 * TOK * SPAN * FEATURES,
            bytes_accessed=5 * TOK * FEATURES * 2,
            transcendentals=2 * HEADS * TOK * SPAN,
        ),
    )(
        section_input[0, 0],
        section_positions[0],
        saved_input[0, 0],
        saved_positions[0],
        cotangent[0, 0],
        norm_gains[:, 0],
        output_gains,
        plan[0],
    )
    return (produced[None, None], grads[None, None], totals.reshape(1, 3, FEATURES))


def solution(mesh):
    placed = (
        P("dp", "pipe", "ctx", None),
        P("dp", "pipe", "ctx"),
        P("dp", "pipe", "ctx", None),
        P("dp", "pipe", "ctx"),
        P("dp", "pipe", "ctx", None),
        P(None, "pipe", None, None),
        P(None, "pipe", None),
        P("dp", "pipe", None),
    )
    return jax.shard_map(
        functools.partial(local, {axis: mesh.shape[axis] for axis in ("dp", "pipe", "ctx")}),
        mesh=mesh,
        in_specs=placed,
        out_specs=(
            P("dp", "pipe", "ctx", None),
            P("dp", "pipe", "ctx", None),
            P("pipe", None, None),
        ),
        check_vma=False,
    )
```
